32 devices in a mesh: rep: 16 (over z, x, core), shard: 2 (over y).
Axes of the slice: x: 2, y: 2, z: 4, core: 2. Of those that a mesh axis runs over, the one named last changes fastest.
Arguments:
- inputs: bfloat16 [32, 512, 576], P(('rep', 'shard')), may hold values from -6 to 6
- segments: int32 [32, 512], P(('rep', 'shard')), may hold values from 0 to 3, never falling along the last dimension, each value on 1 to 256 neighbouring positions
- cotangent: bfloat16 [32, 512, 576], P(('rep', 'shard')), may hold values from -6 to 6
- norm1_gain: bfloat16 [576], P('shard'), may hold values from 0.5 to 1.5
- w_query: bfloat16 [576, 576], P('shard'), may hold values from -0.25 to 0.25
- w_key: bfloat16 [576, 192], P('shard'), may hold values from -0.25 to 0.25
- w_value: bfloat16 [576, 192], P('shard'), may hold values from -0.25 to 0.25
- w_out: bfloat16 [576, 576], P('shard'), may hold values from -1.5 to 1.5
- norm2_gain: bfloat16 [576], P('shard'), may hold values from 0.5 to 1.5
- w_gate: bfloat16 [576, 1536], P('shard'), may hold values from -0.25 to 0.25
- w_up: bfloat16 [576, 1536], P('shard'), may hold values from -0.25 to 0.25
- w_down: bfloat16 [1536, 576], P('shard'), may hold values from -0.15625 to 0.15625
Outputs:
- output: bfloat16 [32, 512, 576], P(('rep', 'shard'))
- input_grad: bfloat16 [32, 512, 576], P(('rep', 'shard'))
- grad_norm1: float32 [576], P('shard')
- grad_query: float32 [576, 576], P('shard')
- grad_key: float32 [576, 192], P('shard')
- grad_value: float32 [576, 192], P('shard')
- grad_out: float32 [576, 576], P('shard')
- grad_norm2: float32 [576], P('shard')
- grad_gate: float32 [576, 1536], P('shard')
- grad_up: float32 [576, 1536], P('shard')
- grad_down: float32 [1536, 576], P('shard')
The draws below stay inside these ranges and needn't reach their ends.
Inputs may be any that keep to these rules, and one draw needn't show every extreme that they name: `segments`: segment numbers never fall along a sequence; each segment has 1 to 256 tokens, one exactly that many.
All inputs are finite; a program needn't handle non-finite values.
Results may differ from the reference program's by a relative error of at most 0.02.
Values may be sent and summed in bfloat16 or wider, within the bound.
A program may use at most 128 MiB of HBM per device.

```python
import math
import jax
import jax.numpy as jnp
import numpy as np
from jax import lax

D = 576
HEADS = 9
KV_HEADS = 3
HEAD_DIM = 64
FF = 1536
TOK_DEV = 512
SEQS = 32


def strengthened(drawn, stream_key, source, target, shards_of, factor):
    def block_of(axis_at):
        return (jnp.arange(drawn.shape[axis_at]) // (drawn.shape[axis_at] // shards_of)).reshape((-1,) + (1,) * (drawn.ndim - 1 - axis_at))

    near = jax.random.permutation(stream_key, shards_of)[block_of(target)]
    other_side = (block_of(target) + shards_of // 2) % shards_of
    return jnp.where((block_of(source) == near) | (block_of(source) == other_side), factor * drawn, drawn)


def level_of(key, dims, shards, least, high):
    def one(dim, blocks):
        heights = jax.random.uniform(jax.random.fold_in(jax.random.fold_in(key, 6), dim), (blocks,), jnp.float32, least / len(shards), high / len(shards))
        return jnp.repeat(jnp.exp(heights), dims[dim] // blocks).reshape((-1,) + (1,) * (len(dims) - dim - 1))

    factor_of = one(*shards[0])
    for cut in shards[1:]:
        factor_of = factor_of * one(*cut)
    return factor_of


def profile(number_of, total, limit, slope):
    loads = [(1 << 20) // math.isqrt(standing ** slope) + 1 for standing in range(2, number_of + 1)]
    surplus, counts = total - limit - (number_of - 1), [1] * (number_of - 1)
    while surplus > 0:
        movable = [i for i in range(number_of - 1) if counts[i] < limit]
        mass, left = sum([loads[i] for i in movable]), surplus
        for i in movable:
            more = min(limit - counts[i], max(1, left * loads[i] // mass), surplus)
            counts[i] = counts[i] + more
            surplus = surplus - more
    return np.array([limit] + counts)


def uneven_parts(key, count, total, limit, lean):
    if count == 2:
        one = jax.random.randint(key, (), max(1, total - limit), min(limit, total - 1) + 1)
        return jnp.stack([one, total - one])
    sizes = jnp.asarray(profile(count, total, limit, lean), jnp.int32)
    couples = (count - 1) // 2
    donor, sink = sizes[1:1 + 2 * couples:2], sizes[2:2 + 2 * couples:2]
    slack = jnp.minimum(donor - 1, limit - sink)
    moved = jax.random.randint(jax.random.fold_in(key, 1), (couples,), 0, 1 << 20) % (slack + 1)
    sizes = sizes.at[1:1 + 2 * couples:2].set(donor - moved).at[2:2 + 2 * couples:2].set(sink + moved)
    return sizes[jax.random.permutation(jax.random.fold_in(key, 2), count)]


def centred(own_key, shape, scale, bound, pieces=(), kind=jnp.bfloat16):
    loudness = level_of(own_key, shape, pieces, -0.22, 0.18) if pieces else 1.0
    values = jax.random.normal(own_key, shape, jnp.float32) * scale * loudness
    return jnp.minimum(jnp.maximum(values, -bound), bound).astype(kind)


def heavy_noise(stream_key, dims, spread, most, shards, heavy, kind=jnp.bfloat16):
    values = spread * jax.random.normal(stream_key, dims, jnp.float32)
    if shards:
        values = values * level_of(stream_key, dims, shards, -0.22, 0.18)
    return jnp.clip(strengthened(values, jax.random.fold_in(stream_key, 3), *heavy), -most, most).astype(kind)


def setup_inputs(seed: int = 0) -> dict:
    seeds = jax.random.split(jax.random.key(seed), 13)
    inputs = heavy_noise(seeds[0], (SEQS, TOK_DEV, D), 1.0, 6.0, ((0, 32),), (0, 2, 32, 2.75))
    segments = jax.vmap(lambda own: jnp.searchsorted(jnp.cumsum(uneven_parts(own, 4, TOK_DEV, TOK_DEV // 2, 1)), jnp.arange(TOK_DEV), side="right"))(jax.random.split(seeds[1], SEQS)).reshape((SEQS, TOK_DEV)).astype(jnp.int32)
    cotangent = centred(seeds[2], (SEQS, TOK_DEV, D), 1.0, 6.0, ((0, 32),))
    norm1_gain = jnp.clip(1.0 + 0.1 * jax.random.normal(seeds[3], (D,), jnp.float32), 0.5, 1.5).astype(jnp.bfloat16)
    w_query = centred(seeds[4], (D, D), D ** -0.5, 0.25, ((0, 2),))
    w_key = centred(seeds[5], (D, KV_HEADS * HEAD_DIM), D ** -0.5, 0.25, ((0, 2),))
    w_value = centred(seeds[6], (D, KV_HEADS * HEAD_DIM), D ** -0.5, 0.25, ((0, 2),))
    w_out = centred(seeds[7], (D, D), (D // 36) ** -0.5, 1.5, ((0, 2),))
    norm2_gain = jnp.clip(1.0 + 0.1 * jax.random.normal(seeds[8], (D,), jnp.float32), 0.5, 1.5).astype(jnp.bfloat16)
    w_gate = centred(seeds[9], (D, FF), D ** -0.5, 0.25, ((0, 2),))
    w_up = centred(seeds[10], (D, FF), D ** -0.5, 0.25, ((0, 2),))
    w_down = centred(seeds[11], (FF, D), FF ** -0.5, 0.15625, ((0, 2),))
    return {"inputs": inputs, "segments": segments, "cotangent": cotangent, "norm1_gain": norm1_gain, "w_query": w_query, "w_key": w_key, "w_value": w_value, "w_out": w_out, "norm2_gain": norm2_gain, "w_gate": w_gate, "w_up": w_up, "w_down": w_down}


@jax.custom_vjp
def low(v):
    return lax.optimization_barrier(v.astype(jnp.bfloat16)).astype(jnp.float32)

@jax.custom_vjp
def low_back(v):
    return v

def low_keep(v):
    return (low(v), None)

def low_pass(kept, grad):
    return (grad,)

def back_keep(v):
    return (v, None)

def back_low(kept, grad):
    return (low(grad),)
low.defvjp(low_keep, low_pass)
low_back.defvjp(back_keep, back_low)
eps = 1e-05
rope_base = 100000.0
highest = lax.Precision.HIGHEST

def rope_tables(seg_row):
    count = seg_row.shape[0]
    index = jnp.arange(count, dtype=jnp.int32)
    before = jnp.concatenate([jnp.full((1,), -1, jnp.int32), seg_row[:-1].astype(jnp.int32)])
    starts = jnp.where(seg_row.astype(jnp.int32) != before, index, jnp.zeros_like(index))
    place = (index - lax.cummax(starts, axis=0)).astype(jnp.float32)
    half = HEAD_DIM // 2
    freqs = jnp.exp(jnp.arange(half, dtype=jnp.float32) * (-2.0 * math.log(rope_base) / HEAD_DIM))
    angle = place[:, None] * freqs[None, :]
    return (jnp.cos(angle), jnp.sin(angle))

def rotate(values, cosine, sine, sign):
    half = HEAD_DIM // 2
    first = values[..., :half]
    second = values[..., half:]
    cos_b = cosine[:, None, :]
    sin_b = sine[:, None, :] * sign
    return jnp.concatenate([first * cos_b - second * sin_b, second * cos_b + first * sin_b], axis=-1)

def layer(x, seg_row, gain_one, wq, wk, wv, wo, gain_two, wg, wu, wd):
    count = x.shape[0]
    group = HEADS // KV_HEADS
    r_one = lax.rsqrt(lax.optimization_barrier(jnp.mean(x * x, axis=1, keepdims=True)) + eps)
    h_one = low(x * r_one * gain_one)
    q_lin = low_back(jnp.dot(h_one, wq, precision=highest))
    k_lin = low_back(jnp.dot(h_one, wk, precision=highest))
    values = low(low_back(jnp.dot(h_one, wv, precision=highest)))
    cosine, sine = rope_tables(seg_row)
    queries = low(rotate(q_lin.reshape(count, HEADS, HEAD_DIM), cosine, sine, 1.0))
    keys = low(rotate(k_lin.reshape(count, KV_HEADS, HEAD_DIM), cosine, sine, 1.0))
    queries = queries.reshape(count, KV_HEADS, group, HEAD_DIM)
    values = values.reshape(count, KV_HEADS, HEAD_DIM)
    dots = jnp.einsum('tkgd,skd->kgts', queries, keys, precision=highest) * HEAD_DIM ** (-0.5)
    index = jnp.arange(count)
    allowed = (seg_row[:, None] == seg_row[None, :]) & (index[:, None] >= index[None, :])
    scores = low_back(jnp.where(allowed, dots, -1e+30))
    top = lax.optimization_barrier(jnp.max(scores, axis=3, keepdims=True))
    expo = jnp.exp(scores - top)
    probs = low(expo / lax.optimization_barrier(jnp.sum(expo, axis=3, keepdims=True)))
    mixed = jnp.einsum('kgts,skd->tkgd', probs, values, precision=highest).reshape(count, D)
    mixed = low(low_back(mixed))
    y_one = x + low_back(jnp.dot(mixed, wo, precision=highest))
    r_two = lax.rsqrt(lax.optimization_barrier(jnp.mean(y_one * y_one, axis=1, keepdims=True)) + eps)
    h_two = low(y_one * r_two * gain_two)
    gate = low_back(jnp.dot(h_two, wg, precision=highest))
    up_val = low_back(jnp.dot(h_two, wu, precision=highest))
    hidden = low(gate * jax.nn.sigmoid(gate) * up_val)
    return y_one + low_back(jnp.dot(hidden, wd, precision=highest))

def reference(inputs, segments, cotangent, norm1_gain, w_query, w_key, w_value, w_out, norm2_gain, w_gate, w_up, w_down):
    params = tuple((w.astype(jnp.float32) for w in (norm1_gain, w_query, w_key, w_value, w_out, norm2_gain, w_gate, w_up, w_down)))
    group_seqs = 8
    blocks = SEQS // group_seqs
    xs = inputs.astype(jnp.float32).reshape(blocks, group_seqs, TOK_DEV, D)
    segs = segments.astype(jnp.int32).reshape(blocks, group_seqs, TOK_DEV)
    cots = cotangent.astype(jnp.float32).reshape(blocks, group_seqs, TOK_DEV, D)

    def step(totals, item):
        x_blk, seg_blk, cot_blk = item

        def forward(x_in, *weights):
            return jax.vmap(lambda row, srow: layer(row, srow, *weights))(x_in, seg_blk)
        result, pull = jax.vjp(forward, x_blk, *params)
        grads = pull(cot_blk)
        totals = tuple((t + g for t, g in zip(totals, grads[1:])))
        return (totals, (result, grads[0]))
    zeros = tuple((jnp.zeros_like(p) for p in params))
    totals, (results, dxs) = lax.scan(step, zeros, (xs, segs, cots))
    output = results.reshape(SEQS, TOK_DEV, D).astype(jnp.bfloat16)
    input_grad = dxs.reshape(SEQS, TOK_DEV, D).astype(jnp.bfloat16)
    return (output, input_grad, totals[0], totals[1], totals[2], totals[3], totals[4], totals[5], totals[6], totals[7], totals[8])
```

```python
import functools
import math

import jax
import jax.numpy as jnp
from jax import lax
from jax.sharding import PartitionSpec as P

HEAD_DIM = 64


eps = 1e-05
rope_base = 100000.0


def rope_tables(seg_row, head_dim):
    count = seg_row.shape[0]
    index = jnp.arange(count, dtype=jnp.int32)
    before = jnp.concatenate([jnp.full((1,), -1, jnp.int32), seg_row[:-1]])
    starts = jnp.where(seg_row != before, index, jnp.zeros_like(index))
    place = (index - lax.cummax(starts, axis=0)).astype(jnp.float32)
    half = head_dim // 2
    freqs = jnp.exp(jnp.arange(half, dtype=jnp.float32) * (-2.0 * math.log(rope_base) / head_dim))
    angle = place[:, None] * freqs[None, :]
    return (jnp.cos(angle), jnp.sin(angle))


def rotate(values, cosine, sine, sign):
    half = values.shape[-1] // 2
    first = values[..., :half]
    second = values[..., half:]
    cos_b = cosine[:, None, :]
    sin_b = sine[:, None, :] * sign
    return jnp.concatenate(
        [first * cos_b - second * sin_b, second * cos_b + first * sin_b], axis=-1
    )


def attention_scores(queries, keys, allowed, scale):
    dots = jnp.einsum("tkgd,skd->kgts", queries, keys, preferred_element_type=jnp.float32) * scale
    return jnp.where(allowed[None, None], dots, -1e30)


def pair_swap(value, axis, size, bit):
    return lax.ppermute(value, axis, [(i, i ^ bit) for i in range(size)])


def bits_of(size):
    return [1 << b for b in range(size.bit_length() - 1)]


def gather_rows(block, shards, reps, share):
    s = lax.axis_index("shard")
    r = lax.axis_index("rep") % share
    rows, cols = block.shape
    piece = rows // share
    cur = lax.dynamic_slice_in_dim(block, r * piece, piece, 0)[None]
    for bit in bits_of(shards):
        cur = jnp.concatenate([cur, pair_swap(cur, "shard", shards, bit)], axis=0)
    cur = cur[1:, None]
    for bit in reversed(bits_of(share)):
        cur = jnp.concatenate([cur, pair_swap(cur, "rep", reps, bit)], axis=1)
    order = [0]
    for bit in reversed(bits_of(share)):
        order = order + [o ^ bit for o in order]
    out = jnp.zeros((shards * rows, cols), block.dtype)
    out = lax.dynamic_update_slice(out, block, (s * rows, 0))
    for t in range(1, shards):
        for j, o in enumerate(order):
            at = (s ^ t) * rows + (r ^ o) * piece
            out = lax.dynamic_update_slice(out, cur[t - 1, j], (at, 0))
    return out


def halves(value, dim, bit_set):
    half = value.shape[dim] // 2
    mine = lax.dynamic_slice_in_dim(value, bit_set * half, half, dim)
    other = lax.dynamic_slice_in_dim(value, (1 - bit_set) * half, half, dim)
    return mine, other


def add(a, b):
    return (a.astype(jnp.float32) + b.astype(jnp.float32)).astype(jnp.bfloat16)


def reduce_grad(grad, shards, reps, by_cols):
    s = lax.axis_index("shard")
    r = lax.axis_index("rep")
    rows, cols = grad.shape
    cur = grad.reshape(shards, rows // shards, cols)
    steps = []
    rep_bits = bits_of(reps)
    for n, bit in enumerate(rep_bits):
        far = n >= max(1, len(rep_bits) - 2)
        steps.append((bit, 2 if far and by_cols else 1))

    def fold(cur, axis, size, bit, dim, index):
        mine, other = halves(cur, dim, (index // bit) % 2)
        return add(mine, pair_swap(other, axis, size, bit))

    cur = fold(cur, "rep", reps, steps[0][0], steps[0][1], r)
    for bit in reversed(bits_of(shards)):
        cur = fold(cur, "shard", shards, bit, 0, s)
    for bit, dim in steps[1:]:
        cur = fold(cur, "rep", reps, bit, dim, r)
    for bit, dim in reversed(steps):
        got = pair_swap(cur, "rep", reps, bit)
        up = (r // bit) % 2 == 1
        cur = jnp.where(
            up, jnp.concatenate([got, cur], axis=dim), jnp.concatenate([cur, got], axis=dim)
        )
    return cur[0].astype(jnp.float32)


def body(
    shards,
    reps,
    inputs,
    segments,
    cotangent,
    norm1_gain,
    w_query,
    w_key,
    w_value,
    w_out,
    norm2_gain,
    w_gate,
    w_up,
    w_down,
):
    share = 4 if reps % 4 == 0 else 1
    w_qkv = jnp.concatenate([w_query, w_key, w_value], axis=1)
    gains = lax.all_gather(jnp.stack([norm1_gain, norm2_gain]), "shard", axis=1, tiled=True)
    gain_one, gain_two = gains[0], gains[1]
    full_qkv = gather_rows(w_qkv, shards, reps, share)
    nq, nk = w_query.shape[1], w_key.shape[1]
    wq, wk, wv = full_qkv[:, :nq], full_qkv[:, nq : nq + nk], full_qkv[:, nq + nk :]
    wo = gather_rows(w_out, shards, reps, share)
    wg = gather_rows(w_gate, shards, reps, share)
    wu = gather_rows(w_up, shards, reps, share)
    wd = gather_rows(w_down, shards, reps, share)
    x = inputs[0].astype(jnp.float32)
    seg_row = segments[0]
    count = x.shape[0]
    width = x.shape[1]
    kv_heads = wk.shape[1] // HEAD_DIM
    heads = wq.shape[1] // HEAD_DIM
    group = heads // kv_heads
    scale = HEAD_DIM ** (-0.5)
    cosine, sine = rope_tables(seg_row, HEAD_DIM)
    index = jnp.arange(count)
    allowed = (seg_row[:, None] == seg_row[None, :]) & (index[:, None] >= index[None, :])
    g_one = gain_one.astype(jnp.float32)
    r_one = lax.rsqrt(jnp.mean(x * x, axis=1, keepdims=True) + eps)
    h_one = (x * r_one * g_one).astype(jnp.bfloat16)
    q_lin = jnp.dot(h_one, wq, preferred_element_type=jnp.float32)
    k_lin = jnp.dot(h_one, wk, preferred_element_type=jnp.float32)
    values = (
        jnp.dot(h_one, wv, preferred_element_type=jnp.float32)
        .astype(jnp.bfloat16)
        .reshape(count, kv_heads, HEAD_DIM)
    )
    queries = (
        rotate(q_lin.reshape(count, heads, HEAD_DIM), cosine, sine, 1.0)
        .astype(jnp.bfloat16)
        .reshape(count, kv_heads, group, HEAD_DIM)
    )
    keys = rotate(k_lin.reshape(count, kv_heads, HEAD_DIM), cosine, sine, 1.0).astype(jnp.bfloat16)
    scores = attention_scores(queries, keys, allowed, scale)
    top = jnp.max(scores, axis=3, keepdims=True)
    expo = jnp.exp(scores - top)
    total = jnp.sum(expo, axis=3, keepdims=True)
    lse = top + jnp.log(total)
    probs = (expo / total).astype(jnp.bfloat16)
    mixed = jnp.einsum("kgts,skd->tkgd", probs, values, preferred_element_type=jnp.float32)
    mixed_b = mixed.reshape(count, width).astype(jnp.bfloat16)
    y_one = x + jnp.dot(mixed_b, wo, preferred_element_type=jnp.float32)
    g_two = gain_two.astype(jnp.float32)
    r_two = lax.rsqrt(jnp.mean(y_one * y_one, axis=1, keepdims=True) + eps)
    h_two = (y_one * r_two * g_two).astype(jnp.bfloat16)
    gate = jnp.dot(h_two, wg, preferred_element_type=jnp.float32)
    up_val = jnp.dot(h_two, wu, preferred_element_type=jnp.float32)
    sigm = jax.nn.sigmoid(gate)
    hidden = (gate * sigm * up_val).astype(jnp.bfloat16)
    output = y_one + jnp.dot(hidden, wd, preferred_element_type=jnp.float32)
    bq, bk, bv, bo, bg, bu, bd = wq, wk, wv, wo, wg, wu, wd
    d_out = cotangent[0].astype(jnp.float32)
    d_out_b = d_out.astype(jnp.bfloat16)
    grad_down = jnp.einsum("tf,td->fd", hidden, d_out_b, preferred_element_type=jnp.float32)
    d_hidden = jnp.einsum("td,fd->tf", d_out_b, bd, preferred_element_type=jnp.float32)
    d_up = (d_hidden * gate * sigm).astype(jnp.bfloat16)
    d_gate = (d_hidden * up_val * sigm * (1.0 + gate * (1.0 - sigm))).astype(jnp.bfloat16)
    grad_gate = jnp.einsum("td,tf->df", h_two, d_gate, preferred_element_type=jnp.float32)
    grad_up = jnp.einsum("td,tf->df", h_two, d_up, preferred_element_type=jnp.float32)
    d_h_two = jnp.einsum("tf,df->td", d_gate, bg, preferred_element_type=jnp.float32) + jnp.einsum(
        "tf,df->td", d_up, bu, preferred_element_type=jnp.float32
    )
    grad_gain_two = jnp.sum(d_h_two * y_one * r_two, axis=0)
    u_two = d_h_two * g_two
    d_y_one = (
        d_out + r_two * u_two - y_one * r_two**3 * jnp.mean(u_two * y_one, axis=1, keepdims=True)
    )
    d_attn = d_y_one.astype(jnp.bfloat16)
    grad_wo = jnp.einsum("td,te->de", mixed_b, d_attn, preferred_element_type=jnp.float32)
    d_mixed = (
        jnp.einsum("te,de->td", d_attn, bo, preferred_element_type=jnp.float32)
        .astype(jnp.bfloat16)
        .reshape(count, kv_heads, group, HEAD_DIM)
    )
    probs_f = jnp.exp(attention_scores(queries, keys, allowed, scale) - lse)
    probs_b = probs_f.astype(jnp.bfloat16)
    d_probs = jnp.einsum("tkgd,skd->kgts", d_mixed, values, preferred_element_type=jnp.float32)
    delta = jnp.sum(d_probs * probs_f, axis=3, keepdims=True)
    d_scores = (probs_f * (d_probs - delta)).astype(jnp.bfloat16)
    d_queries = (
        jnp.einsum("kgts,skd->tkgd", d_scores, keys, preferred_element_type=jnp.float32) * scale
    )
    d_keys = (
        jnp.einsum("kgts,tkgd->skd", d_scores, queries, preferred_element_type=jnp.float32) * scale
    )
    d_values = jnp.einsum("kgts,tkgd->skd", probs_b, d_mixed, preferred_element_type=jnp.float32)
    dq_b = (
        rotate(d_queries.reshape(count, heads, HEAD_DIM), cosine, sine, -1.0)
        .reshape(count, width)
        .astype(jnp.bfloat16)
    )
    dk_b = (
        rotate(d_keys, cosine, sine, -1.0).reshape(count, kv_heads * HEAD_DIM).astype(jnp.bfloat16)
    )
    dv_b = d_values.reshape(count, kv_heads * HEAD_DIM).astype(jnp.bfloat16)
    grad_wq = jnp.einsum("td,te->de", h_one, dq_b, preferred_element_type=jnp.float32)
    grad_wk = jnp.einsum("td,te->de", h_one, dk_b, preferred_element_type=jnp.float32)
    grad_wv = jnp.einsum("td,te->de", h_one, dv_b, preferred_element_type=jnp.float32)
    d_h_one = jnp.einsum("te,de->td", dq_b, bq, preferred_element_type=jnp.float32)
    d_h_one = d_h_one + jnp.einsum("te,de->td", dk_b, bk, preferred_element_type=jnp.float32)
    d_h_one = d_h_one + jnp.einsum("te,de->td", dv_b, bv, preferred_element_type=jnp.float32)
    grad_gain_one = jnp.sum(d_h_one * x * r_one, axis=0)
    u_one = d_h_one * g_one
    d_x = d_y_one + r_one * u_one - x * r_one**3 * jnp.mean(u_one * x, axis=1, keepdims=True)
    low = jnp.bfloat16
    t_down = reduce_grad(grad_down.astype(low), shards, reps, False)
    t_gate = reduce_grad(grad_gate.astype(low), shards, reps, True)
    t_up = reduce_grad(grad_up.astype(low), shards, reps, True)
    g_attn = jnp.concatenate([grad_wq, grad_wk, grad_wv, grad_wo], axis=1).astype(low)
    t_attn = reduce_grad(g_attn, shards, reps, True)
    g_gains = lax.psum(jnp.stack([grad_gain_one, grad_gain_two]), ("rep", "shard"))
    own = width // shards
    g_gains = lax.dynamic_slice_in_dim(g_gains, lax.axis_index("shard") * own, own, 1)
    return (
        output.astype(low)[None],
        d_x.astype(low)[None],
        g_gains[0],
        t_attn[:, :nq],
        t_attn[:, nq : nq + nk],
        t_attn[:, nq + nk : nq + 2 * nk],
        t_attn[:, nq + 2 * nk :],
        g_gains[1],
        t_gate,
        t_up,
        t_down,
    )


def solution(mesh):
    return jax.shard_map(
        functools.partial(body, mesh.shape["shard"], mesh.shape["rep"]),
        mesh=mesh,
        in_specs=(
            P(("rep", "shard"), None, None),
            P(("rep", "shard"), None),
            P(("rep", "shard"), None, None),
            P("shard"),
            P("shard", None),
            P("shard", None),
            P("shard", None),
            P("shard", None),
            P("shard"),
            P("shard", None),
            P("shard", None),
            P("shard", None),
        ),
        out_specs=(
            P(("rep", "shard"), None, None),
            P(("rep", "shard"), None, None),
            P("shard"),
            P("shard", None),
            P("shard", None),
            P("shard", None),
            P("shard", None),
            P("shard"),
            P("shard", None),
            P("shard", None),
            P("shard", None),
        ),
        check_vma=False,
    )
```

```python
import functools
import math

import jax
import jax.numpy as jnp
from jax import lax
from jax.experimental import pallas as pl
from jax.experimental.pallas import tpu as pltpu
from jax.sharding import PartitionSpec as P

HEAD_DIM = 64
MESH = pl.DeviceIdType.MESH
VMEM_LIMIT = 48 * 1024 * 1024


eps = 1e-05
rope_base = 100000.0


def rope_tables(seg_row, head_dim):
    count = seg_row.shape[0]
    index = jnp.arange(count, dtype=jnp.int32)
    before = jnp.concatenate([jnp.full((1,), -1, jnp.int32), seg_row[:-1]])
    starts = jnp.where(seg_row != before, index, jnp.zeros_like(index))
    place = (index - lax.cummax(starts, axis=0)).astype(jnp.float32)
    half = head_dim // 2
    freqs = jnp.exp(jnp.arange(half, dtype=jnp.float32) * (-2.0 * math.log(rope_base) / head_dim))
    angle = place[:, None] * freqs[None, :]
    return (jnp.cos(angle), jnp.sin(angle))


def rotate(values, cosine, sine, sign):
    half = values.shape[-1] // 2
    first = values[..., :half]
    second = values[..., half:]
    cos_b = cosine[:, None, :]
    sin_b = sine[:, None, :] * sign
    return jnp.concatenate(
        [first * cos_b - second * sin_b, second * cos_b + first * sin_b], axis=-1
    )


def attention_scores(queries, keys, allowed, scale):
    dots = jnp.einsum("tkgd,skd->kgts", queries, keys, preferred_element_type=jnp.float32) * scale
    return jnp.where(allowed[None, None], dots, -1e30)


def bits_of(size):
    return [1 << b for b in range(size.bit_length() - 1)]


def flipped(index, bit):
    return index + bit - 2 * bit * ((index // bit) % 2)


def greet(partners):
    barrier = pltpu.get_barrier_semaphore()
    for partner in partners:
        pl.semaphore_signal(barrier, inc=1, device_id=partner, device_id_type=MESH)
    pl.semaphore_wait(barrier, len(partners))


def gather_kernel(shards, share, dims, *refs):
    count = len(dims)
    blocks, outs = refs[:count], refs[count : 2 * count]
    send, recv, local = refs[2 * count :]
    r, s = lax.axis_index("rep"), lax.axis_index("shard")
    bits = list(reversed(bits_of(share)))
    others = [lax.rem(s + t, shards) for t in range(1, shards)]
    back = [lax.rem(s + shards - t, shards) for t in range(1, shards)]
    greet([(r, o) for o in others] + [(flipped(r, bit), s) for bit in bits])

    def part(ref, dim, owner):
        if dim is None:
            return (slice(None), slice(None))
        size = ref.shape[dim - (3 - len(ref.shape))] // share
        cut = pl.ds(pl.multiple_of(owner * size, size), size)
        return (cut, slice(None)) if dim == 1 else (slice(None), cut)

    held = {}
    copies, stays = [], []
    for a in range(count):
        own = pltpu.make_async_copy(blocks[a], outs[a].at[s], local.at[a])
        own.start()
        stays.append(own)
        held[a] = [lax.rem(r, share)]
        for t in range(1, shards):
            cut = part(blocks[a], dims[a], held[a][0])
            go = pltpu.make_async_remote_copy(
                src_ref=blocks[a].at[cut],
                dst_ref=outs[a].at[(s,) + cut],
                send_sem=send.at[a, t - 1, 0],
                recv_sem=recv.at[a, t - 1, 0],
                device_id=(r, others[t - 1]),
                device_id_type=MESH,
            )
            go.start()
            held[a, t] = [go]
    pending = {}
    for tick in range(count + len(bits)):
        for a in range(count):
            level = tick - a
            if dims[a] is None or not 0 <= level < len(bits):
                continue
            bit = bits[level]
            fresh = []
            for t in range(1, shards):
                arrived = held[a, t] if level == 0 else pending[a, t]
                for go in arrived:
                    go.wait_recv()
                now = []
                for j in range(1 << level):
                    owner = held[a][j]
                    cut = part(blocks[a], dims[a], owner)
                    where = outs[a].at[(back[t - 1],) + cut]
                    go = pltpu.make_async_remote_copy(
                        src_ref=where,
                        dst_ref=where,
                        send_sem=send.at[a, t - 1, (1 << level) + j],
                        recv_sem=recv.at[a, t - 1, (1 << level) + j],
                        device_id=(flipped(r, bit), s),
                        device_id_type=MESH,
                    )
                    go.start()
                    now.append(go)
                pending[a, t] = now
                copies.extend(arrived)
            held[a] = held[a] + [flipped(o, bit) for o in held[a]]
    for a in range(count):
        for t in range(1, shards):
            last = pending.get((a, t), held[a, t])
            for go in last:
                go.wait_recv()
            copies.extend(last)
    for go in copies:
        go.wait_send()
    for own in stays:
        own.wait()


def gather_weights(blocks, dims, shards, share):
    return pl.pallas_call(
        functools.partial(gather_kernel, shards, share, dims),
        out_shape=[jax.ShapeDtypeStruct((shards,) + b.shape, b.dtype) for b in blocks],
        in_specs=[pl.BlockSpec(memory_space=pltpu.VMEM)] * len(blocks),
        out_specs=[pl.BlockSpec(memory_space=pltpu.VMEM)] * len(blocks),
        scratch_shapes=[
            pltpu.SemaphoreType.DMA((len(blocks), max(1, shards - 1), share)),
            pltpu.SemaphoreType.DMA((len(blocks), max(1, shards - 1), share)),
            pltpu.SemaphoreType.DMA((len(blocks),)),
        ],
        compiler_params=pltpu.CompilerParams(
            collective_id=0, has_side_effects=True, vmem_limit_bytes=VMEM_LIMIT
        ),
    )(*blocks)


def plan_of(shape, shards, reps, splits):
    rep_bits, shard_bits = bits_of(reps), list(reversed(bits_of(shards)))
    size = list(shape)
    order = [("rep", rep_bits[0])] + [("shard", b) for b in shard_bits]
    order += [("rep", b) for b in rep_bits[1:]]
    steps = []
    for n, (axis, bit) in enumerate(order):
        dim = None
        if splits and axis == "shard":
            dim = 0
        elif splits and n < len(order) - 1:
            if size[1] % 32 == 0 and (size[2] % 256 != 0 or n == 0):
                dim = 1
            elif size[2] % 256 == 0:
                dim = 2
        if dim is not None:
            size[dim] //= 2
        steps.append((axis, bit, dim, tuple(size)))
    return steps


def reduce_kernel(plans, shards, count, *refs):
    grads, outs = refs[:count], refs[count : 2 * count]
    refs = refs[2 * count :]
    send, recv = refs[-2:]
    lands, at = [], 0
    for plan in plans:
        lands.append(refs[at : at + len(plan)])
        at += len(plan)
    r, s = lax.axis_index("rep"), lax.axis_index("shard")
    index = {"rep": r, "shard": s}

    def partner(axis, bit):
        return (flipped(r, bit), s) if axis == "rep" else (r, flipped(s, bit))

    greet([partner(axis, bit) for axis, bit, _, _ in plans[0]])

    def half(shape, dim, which):
        cut = [slice(None)] * 3
        size = shape[dim] // 2
        start = which * size
        cut[dim] = pl.ds(start if dim == 0 else pl.multiple_of(start, size), size)
        return tuple(cut)

    waits = []

    def start(c, n, src, dst, axis, bit):
        go = pltpu.make_async_remote_copy(
            src_ref=src,
            dst_ref=dst,
            send_sem=send.at[c, n],
            recv_sem=recv.at[c, n],
            device_id=partner(axis, bit),
            device_id_type=MESH,
        )
        go.start()
        waits.append(go)
        return go

    def stream(c):
        plan, cur = plans[c], grads[c]
        offset = [0, 0, 0]
        shape = cur.shape
        n = 0
        for step, (axis, bit, dim, after) in enumerate(plan):
            land = lands[c][step]
            on = (index[axis] // bit) % 2
            if dim is None:
                go = start(c, n, cur, land, axis, bit)
                yield
                go.wait_recv()
                land[...] = cur[...] + land[...]
            else:
                theirs = half(shape, dim, 1 - on)
                mine = half(shape, dim, on)
                go = start(c, n, cur.at[theirs], land, axis, bit)
                yield
                go.wait_recv()
                land[...] = cur[mine] + land[...]
                if axis == "rep":
                    offset[dim] = offset[dim] + on * after[dim]
            cur, shape = land, after
            n += 1
        out = outs[c]

        def place(offset, size):
            cut = []
            for d in (1, 2):
                if size[d] == out.shape[d]:
                    cut.append(slice(None))
                else:
                    unit = 16 if d == 1 else 128
                    cut.append(pl.ds(pl.multiple_of(offset[d], unit), size[d]))
            return (slice(None),) + tuple(cut)

        size = list(shape)
        out[place(offset, size)] = cur[...]
        for axis, bit, dim, after in reversed(plan):
            if axis == "shard" or dim is None:
                continue
            block = out.at[place(offset, size)]
            go = start(c, n, block, block, axis, bit)
            yield
            go.wait_recv()
            on = (index[axis] // bit) % 2
            offset[dim] = offset[dim] - on * after[dim]
            size[dim] *= 2
            n += 1

    streams = [stream(c) for c in range(count)]
    live = []
    while streams or live:
        if streams:
            live.append(streams.pop(0))
        for one in list(live):
            try:
                next(one)
            except StopIteration:
                live.remove(one)
    for go in waits:
        go.wait_send()


def reduce_grads(grads, splits, shards, reps):
    plans = [plan_of(g.shape, shards, reps, cut) for g, cut in zip(grads, splits)]
    outs, lands, most = [], [], 0
    for g, plan, cut in zip(grads, plans, splits):
        lead = 1 if cut else g.shape[0]
        outs.append(jax.ShapeDtypeStruct((lead,) + g.shape[1:], g.dtype))
        lands += [pltpu.VMEM(after, g.dtype) for _, _, _, after in plan]
        most = max(most, 2 * len(plan))
    return pl.pallas_call(
        functools.partial(reduce_kernel, plans, shards, len(grads)),
        out_shape=outs,
        in_specs=[pl.BlockSpec(memory_space=pltpu.VMEM)] * len(grads),
        out_specs=[pl.BlockSpec(memory_space=pltpu.VMEM)] * len(grads),
        scratch_shapes=lands
        + [
            pltpu.SemaphoreType.DMA((len(grads), most)),
            pltpu.SemaphoreType.DMA((len(grads), most)),
        ],
        compiler_params=pltpu.CompilerParams(
            collective_id=1, has_side_effects=True, vmem_limit_bytes=VMEM_LIMIT
        ),
    )(*grads)


def body(
    shards,
    reps,
    inputs,
    segments,
    cotangent,
    norm1_gain,
    w_query,
    w_key,
    w_value,
    w_out,
    norm2_gain,
    w_gate,
    w_up,
    w_down,
):
    share = 4 if reps % 4 == 0 else 1
    w_attn = jnp.concatenate([w_query, w_key, w_value, w_out], axis=1)
    w_gain = jnp.zeros((16, norm1_gain.shape[0]), norm1_gain.dtype)
    w_gain = w_gain.at[0].set(norm1_gain).at[1].set(norm2_gain)
    nq, nk = w_query.shape[1], w_key.shape[1]
    w_all = gather_weights(
        [w_attn, w_gate, w_up, w_down, w_gain], [2, 2, 2, 1, None], shards, share
    )
    wa, wg, wu, wd = [w.reshape(-1, w.shape[2]) for w in w_all[:4]]
    gain_one, gain_two = w_all[4][:, 0].reshape(-1), w_all[4][:, 1].reshape(-1)
    wq, wk, wv = wa[:, :nq], wa[:, nq : nq + nk], wa[:, nq + nk : nq + 2 * nk]
    wo = wa[:, nq + 2 * nk :]
    x = inputs[0].astype(jnp.float32)
    seg_row = segments[0]
    count = x.shape[0]
    width = x.shape[1]
    kv_heads = wk.shape[1] // HEAD_DIM
    heads = wq.shape[1] // HEAD_DIM
    group = heads // kv_heads
    scale = HEAD_DIM ** (-0.5)
    cosine, sine = rope_tables(seg_row, HEAD_DIM)
    index = jnp.arange(count)
    allowed = (seg_row[:, None] == seg_row[None, :]) & (index[:, None] >= index[None, :])
    g_one = gain_one.astype(jnp.float32)
    r_one = lax.rsqrt(jnp.mean(x * x, axis=1, keepdims=True) + eps)
    h_one = (x * r_one * g_one).astype(jnp.bfloat16)
    q_lin = jnp.dot(h_one, wq, preferred_element_type=jnp.float32)
    k_lin = jnp.dot(h_one, wk, preferred_element_type=jnp.float32)
    values = (
        jnp.dot(h_one, wv, preferred_element_type=jnp.float32)
        .astype(jnp.bfloat16)
        .reshape(count, kv_heads, HEAD_DIM)
    )
    queries = (
        rotate(q_lin.reshape(count, heads, HEAD_DIM), cosine, sine, 1.0)
        .astype(jnp.bfloat16)
        .reshape(count, kv_heads, group, HEAD_DIM)
    )
    keys = rotate(k_lin.reshape(count, kv_heads, HEAD_DIM), cosine, sine, 1.0).astype(jnp.bfloat16)
    scores = attention_scores(queries, keys, allowed, scale)
    top = jnp.max(scores, axis=3, keepdims=True)
    expo = jnp.exp(scores - top)
    total = jnp.sum(expo, axis=3, keepdims=True)
    lse = top + jnp.log(total)
    probs = (expo / total).astype(jnp.bfloat16)
    mixed = jnp.einsum("kgts,skd->tkgd", probs, values, preferred_element_type=jnp.float32)
    mixed_b = mixed.reshape(count, width).astype(jnp.bfloat16)
    y_one = x + jnp.dot(mixed_b, wo, preferred_element_type=jnp.float32)
    g_two = gain_two.astype(jnp.float32)
    r_two = lax.rsqrt(jnp.mean(y_one * y_one, axis=1, keepdims=True) + eps)
    h_two = (y_one * r_two * g_two).astype(jnp.bfloat16)
    gate = jnp.dot(h_two, wg, preferred_element_type=jnp.float32)
    up_val = jnp.dot(h_two, wu, preferred_element_type=jnp.float32)
    sigm = jax.nn.sigmoid(gate)
    hidden = (gate * sigm * up_val).astype(jnp.bfloat16)
    output = y_one + jnp.dot(hidden, wd, preferred_element_type=jnp.float32)
    bq, bk, bv, bo, bg, bu, bd = wq, wk, wv, wo, wg, wu, wd
    d_out = cotangent[0].astype(jnp.float32)
    d_out_b = d_out.astype(jnp.bfloat16)
    grad_down = jnp.einsum("tf,td->fd", hidden, d_out_b, preferred_element_type=jnp.float32)
    d_hidden = jnp.einsum("td,fd->tf", d_out_b, bd, preferred_element_type=jnp.float32)
    d_up = (d_hidden * gate * sigm).astype(jnp.bfloat16)
    d_gate = (d_hidden * up_val * sigm * (1.0 + gate * (1.0 - sigm))).astype(jnp.bfloat16)
    grad_gate = jnp.einsum("td,tf->df", h_two, d_gate, preferred_element_type=jnp.float32)
    grad_up = jnp.einsum("td,tf->df", h_two, d_up, preferred_element_type=jnp.float32)
    d_h_two = jnp.einsum("tf,df->td", d_gate, bg, preferred_element_type=jnp.float32) + jnp.einsum(
        "tf,df->td", d_up, bu, preferred_element_type=jnp.float32
    )
    grad_gain_two = jnp.sum(d_h_two * y_one * r_two, axis=0)
    u_two = d_h_two * g_two
    d_y_one = (
        d_out + r_two * u_two - y_one * r_two**3 * jnp.mean(u_two * y_one, axis=1, keepdims=True)
    )
    d_attn = d_y_one.astype(jnp.bfloat16)
    grad_wo = jnp.einsum("td,te->de", mixed_b, d_attn, preferred_element_type=jnp.float32)
    d_mixed = (
        jnp.einsum("te,de->td", d_attn, bo, preferred_element_type=jnp.float32)
        .astype(jnp.bfloat16)
        .reshape(count, kv_heads, group, HEAD_DIM)
    )
    probs_f = jnp.exp(attention_scores(queries, keys, allowed, scale) - lse)
    probs_b = probs_f.astype(jnp.bfloat16)
    d_probs = jnp.einsum("tkgd,skd->kgts", d_mixed, values, preferred_element_type=jnp.float32)
    delta = jnp.sum(d_probs * probs_f, axis=3, keepdims=True)
    d_scores = (probs_f * (d_probs - delta)).astype(jnp.bfloat16)
    d_queries = (
        jnp.einsum("kgts,skd->tkgd", d_scores, keys, preferred_element_type=jnp.float32) * scale
    )
    d_keys = (
        jnp.einsum("kgts,tkgd->skd", d_scores, queries, preferred_element_type=jnp.float32) * scale
    )
    d_values = jnp.einsum("kgts,tkgd->skd", probs_b, d_mixed, preferred_element_type=jnp.float32)
    dq_b = (
        rotate(d_queries.reshape(count, heads, HEAD_DIM), cosine, sine, -1.0)
        .reshape(count, width)
        .astype(jnp.bfloat16)
    )
    dk_b = (
        rotate(d_keys, cosine, sine, -1.0).reshape(count, kv_heads * HEAD_DIM).astype(jnp.bfloat16)
    )
    dv_b = d_values.reshape(count, kv_heads * HEAD_DIM).astype(jnp.bfloat16)
    grad_wq = jnp.einsum("td,te->de", h_one, dq_b, preferred_element_type=jnp.float32)
    grad_wk = jnp.einsum("td,te->de", h_one, dk_b, preferred_element_type=jnp.float32)
    grad_wv = jnp.einsum("td,te->de", h_one, dv_b, preferred_element_type=jnp.float32)
    d_h_one = jnp.einsum("te,de->td", dq_b, bq, preferred_element_type=jnp.float32)
    d_h_one = d_h_one + jnp.einsum("te,de->td", dk_b, bk, preferred_element_type=jnp.float32)
    d_h_one = d_h_one + jnp.einsum("te,de->td", dv_b, bv, preferred_element_type=jnp.float32)
    grad_gain_one = jnp.sum(d_h_one * x * r_one, axis=0)
    u_one = d_h_one * g_one
    d_x = d_y_one + r_one * u_one - x * r_one**3 * jnp.mean(u_one * x, axis=1, keepdims=True)
    low = jnp.bfloat16
    g_attn = jnp.concatenate([grad_wq, grad_wk, grad_wv, grad_wo], axis=1)
    g_gains = jnp.zeros((1, 8, width), jnp.float32)
    g_gains = g_gains.at[0, 0].set(grad_gain_one).at[0, 1].set(grad_gain_two)
    parts = [
        g.astype(low).reshape(shards, -1, g.shape[1])
        for g in (grad_down, grad_gate, grad_up, g_attn)
    ]
    sums = reduce_grads(parts + [g_gains], [True] * 4 + [False], shards, reps)
    t_down, t_gate, t_up, t_attn = [t[0].astype(jnp.float32) for t in sums[:4]]
    g_gains = sums[4][0, :2]
    own = width // shards
    g_gains = lax.dynamic_slice_in_dim(g_gains, lax.axis_index("shard") * own, own, 1)
    return (
        output.astype(low)[None],
        d_x.astype(low)[None],
        g_gains[0],
        t_attn[:, :nq],
        t_attn[:, nq : nq + nk],
        t_attn[:, nq + nk : nq + 2 * nk],
        t_attn[:, nq + 2 * nk :],
        g_gains[1],
        t_gate,
        t_up,
        t_down,
    )


def solution(mesh):
    return jax.shard_map(
        functools.partial(body, mesh.shape["shard"], mesh.shape["rep"]),
        mesh=mesh,
        in_specs=(
            P(("rep", "shard"), None, None),
            P(("rep", "shard"), None),
            P(("rep", "shard"), None, None),
            P("shard"),
            P("shard", None),
            P("shard", None),
            P("shard", None),
            P("shard", None),
            P("shard"),
            P("shard", None),
            P("shard", None),
            P("shard", None),
        ),
        out_specs=(
            P(("rep", "shard"), None, None),
            P(("rep", "shard"), None, None),
            P("shard"),
            P("shard", None),
            P("shard", None),
            P("shard", None),
            P("shard", None),
            P("shard"),
            P("shard", None),
            P("shard", None),
            P("shard", None),
        ),
        check_vma=False,
    )
```

```python
import functools
import math

import jax
import jax.numpy as jnp
from jax import lax
from jax.experimental import pallas as pl
from jax.experimental.pallas import tpu as pltpu
from jax.sharding import PartitionSpec as P

HEAD_DIM = 64
MESH = pl.DeviceIdType.MESH
VMEM_LIMIT = 48 * 1024 * 1024


eps = 1e-05
rope_base = 100000.0


def rope_tables(seg_row, head_dim):
    count = seg_row.shape[0]
    index = jnp.arange(count, dtype=jnp.int32)
    before = jnp.concatenate([jnp.full((1,), -1, jnp.int32), seg_row[:-1]])
    starts = jnp.where(seg_row != before, index, jnp.zeros_like(index))
    place = (index - lax.cummax(starts, axis=0)).astype(jnp.float32)
    half = head_dim // 2
    freqs = jnp.exp(jnp.arange(half, dtype=jnp.float32) * (-2.0 * math.log(rope_base) / head_dim))
    angle = place[:, None] * freqs[None, :]
    return (jnp.cos(angle), jnp.sin(angle))


def rotate(values, cosine, sine, sign):
    half = values.shape[-1] // 2
    first = values[..., :half]
    second = values[..., half:]
    cos_b = cosine[:, None, :]
    sin_b = sine[:, None, :] * sign
    return jnp.concatenate(
        [first * cos_b - second * sin_b, second * cos_b + first * sin_b], axis=-1
    )


def attention_scores(queries, keys, allowed, scale):
    dots = jnp.einsum("tkgd,skd->kgts", queries, keys, preferred_element_type=jnp.float32) * scale
    return jnp.where(allowed[None, None], dots, -1e30)


def bits_of(size):
    return [1 << b for b in range(size.bit_length() - 1)]


def flipped(index, bit):
    return index + bit - 2 * bit * ((index // bit) % 2)


def greet(partners):
    barrier = pltpu.get_barrier_semaphore()
    for partner in partners:
        pl.semaphore_signal(barrier, inc=1, device_id=partner, device_id_type=MESH)
    pl.semaphore_wait(barrier, len(partners))


def gather_kernel(shards, share, dims, *refs):
    count = len(dims)
    blocks, outs = refs[:count], refs[count : 2 * count]
    send, recv, local = refs[2 * count :]
    r, s = lax.axis_index("rep"), lax.axis_index("shard")
    bits = list(reversed(bits_of(share)))
    others = [lax.rem(s + t, shards) for t in range(1, shards)]
    back = [lax.rem(s + shards - t, shards) for t in range(1, shards)]
    greet([(r, o) for o in others] + [(flipped(r, bit), s) for bit in bits])

    def part(ref, dim, owner):
        if dim is None:
            return (slice(None), slice(None))
        size = ref.shape[dim - (3 - len(ref.shape))] // share
        cut = pl.ds(pl.multiple_of(owner * size, size), size)
        return (cut, slice(None)) if dim == 1 else (slice(None), cut)

    held = {}
    copies, stays = [], []
    for a in range(count):
        own = pltpu.make_async_copy(blocks[a], outs[a].at[s], local.at[a])
        own.start()
        stays.append(own)
        held[a] = [lax.rem(r, share)]
        for t in range(1, shards):
            cut = part(blocks[a], dims[a], held[a][0])
            go = pltpu.make_async_remote_copy(
                src_ref=blocks[a].at[cut],
                dst_ref=outs[a].at[(s,) + cut],
                send_sem=send.at[a, t - 1, 0],
                recv_sem=recv.at[a, t - 1, 0],
                device_id=(r, others[t - 1]),
                device_id_type=MESH,
            )
            go.start()
            held[a, t] = [go]
    pending = {}
    for tick in range(count + len(bits)):
        for a in range(count):
            level = tick - a
            if dims[a] is None or not 0 <= level < len(bits):
                continue
            bit = bits[level]
            fresh = []
            for t in range(1, shards):
                arrived = held[a, t] if level == 0 else pending[a, t]
                for go in arrived:
                    go.wait_recv()
                now = []
                for j in range(1 << level):
                    owner = held[a][j]
                    cut = part(blocks[a], dims[a], owner)
                    where = outs[a].at[(back[t - 1],) + cut]
                    go = pltpu.make_async_remote_copy(
                        src_ref=where,
                        dst_ref=where,
                        send_sem=send.at[a, t - 1, (1 << level) + j],
                        recv_sem=recv.at[a, t - 1, (1 << level) + j],
                        device_id=(flipped(r, bit), s),
                        device_id_type=MESH,
                    )
                    go.start()
                    now.append(go)
                pending[a, t] = now
                copies.extend(arrived)
            held[a] = held[a] + [flipped(o, bit) for o in held[a]]
    for a in range(count):
        for t in range(1, shards):
            last = pending.get((a, t), held[a, t])
            for go in last:
                go.wait_recv()
            copies.extend(last)
    for go in copies:
        go.wait_send()
    for own in stays:
        own.wait()


def gather_weights(blocks, dims, shards, share):
    return pl.pallas_call(
        functools.partial(gather_kernel, shards, share, dims),
        out_shape=[jax.ShapeDtypeStruct((shards,) + b.shape, b.dtype) for b in blocks],
        in_specs=[pl.BlockSpec(memory_space=pltpu.VMEM)] * len(blocks),
        out_specs=[pl.BlockSpec(memory_space=pltpu.VMEM)] * len(blocks),
        scratch_shapes=[
            pltpu.SemaphoreType.DMA((len(blocks), max(1, shards - 1), share)),
            pltpu.SemaphoreType.DMA((len(blocks), max(1, shards - 1), share)),
            pltpu.SemaphoreType.DMA((len(blocks),)),
        ],
        compiler_params=pltpu.CompilerParams(
            collective_id=0, has_side_effects=True, vmem_limit_bytes=VMEM_LIMIT
        ),
    )(*blocks)


def plan_of(shape, shards, reps, splits, turn):
    rep_bits, shard_bits = bits_of(reps), list(reversed(bits_of(shards)))
    size = list(shape)
    order = [("rep", b) for b in rep_bits]
    first = 2 if turn % 2 else 1
    order[first:first] = [("shard", b) for b in shard_bits]
    steps = []
    for n, (axis, bit) in enumerate(order):
        dim = None
        if splits and axis == "shard":
            dim = 0
        elif splits and n < len(order) - 1:
            if size[1] % 32 == 0 and (size[2] % 256 != 0 or n == 0):
                dim = 1
            elif size[2] % 256 == 0:
                dim = 2
        if dim is not None:
            size[dim] //= 2
        steps.append((axis, bit, dim, tuple(size)))
    return steps


def reduce_kernel(plans, shards, count, *refs):
    grads, outs = refs[:count], refs[count : 2 * count]
    refs = refs[2 * count :]
    send, recv = refs[-2:]
    lands, at = [], 0
    for plan in plans:
        lands.append(refs[at : at + len(plan)])
        at += len(plan)
    r, s = lax.axis_index("rep"), lax.axis_index("shard")
    index = {"rep": r, "shard": s}

    def partner(axis, bit):
        return (flipped(r, bit), s) if axis == "rep" else (r, flipped(s, bit))

    greet([partner(axis, bit) for axis, bit, _, _ in plans[0]])

    def half(shape, dim, which):
        cut = [slice(None)] * 3
        size = shape[dim] // 2
        start = which * size
        cut[dim] = pl.ds(start if dim == 0 else pl.multiple_of(start, size), size)
        return tuple(cut)

    waits, free, clock = [], {}, [0.0]

    def start(c, n, src, dst, axis, bit):
        go = pltpu.make_async_remote_copy(
            src_ref=src,
            dst_ref=dst,
            send_sem=send.at[c, n],
            recv_sem=recv.at[c, n],
            device_id=partner(axis, bit),
            device_id_type=MESH,
        )
        go.start()
        waits.append(go)
        link = (axis, bit)
        rate = 300e3 if link == ("rep", 1) else 50e3
        begin = max(clock[0], free.get(link, 0.0))
        free[link] = begin + math.prod(src.shape) * 2 / rate
        return go, free[link] + 1.5

    def stream(c):
        plan, cur = plans[c], grads[c]
        offset = [0, 0, 0]
        shape = cur.shape
        n = 0
        for step, (axis, bit, dim, after) in enumerate(plan):
            land = lands[c][step]
            on = (index[axis] // bit) % 2
            if dim is None:
                go, due = start(c, n, cur, land, axis, bit)
                yield due
                go.wait_recv()
                land[...] = cur[...] + land[...]
            else:
                theirs = half(shape, dim, 1 - on)
                mine = half(shape, dim, on)
                go, due = start(c, n, cur.at[theirs], land, axis, bit)
                yield due
                go.wait_recv()
                land[...] = cur[mine] + land[...]
                if axis == "rep":
                    offset[dim] = offset[dim] + on * after[dim]
            cur, shape = land, after
            n += 1
        out = outs[c]

        def place(offset, size):
            cut = []
            for d in (1, 2):
                if size[d] == out.shape[d]:
                    cut.append(slice(None))
                else:
                    unit = 16 if d == 1 else 128
                    cut.append(pl.ds(pl.multiple_of(offset[d], unit), size[d]))
            return (slice(None),) + tuple(cut)

        size = list(shape)
        out[place(offset, size)] = cur[...]
        for axis, bit, dim, after in reversed(plan):
            if axis == "shard" or dim is None:
                continue
            block = out.at[place(offset, size)]
            go, due = start(c, n, block, block, axis, bit)
            yield due
            go.wait_recv()
            on = (index[axis] // bit) % 2
            offset[dim] = offset[dim] - on * after[dim]
            size[dim] *= 2
            n += 1

    streams = [stream(c) for c in range(count)]
    due = [(next(one), c) for c, one in enumerate(streams)]
    while due:
        due.sort()
        clock[0], c = due.pop(0)
        then = next(streams[c], None)
        if then is not None:
            due.append((then, c))
    for go in waits:
        go.wait_send()


def reduce_grads(grads, splits, shards, reps):
    plans = [plan_of(g.shape, shards, reps, cut, i) for i, (g, cut) in enumerate(zip(grads, splits))]
    outs, lands, most = [], [], 0
    for g, plan, cut in zip(grads, plans, splits):
        lead = 1 if cut else g.shape[0]
        outs.append(jax.ShapeDtypeStruct((lead,) + g.shape[1:], g.dtype))
        lands += [pltpu.VMEM(after, g.dtype) for _, _, _, after in plan]
        most = max(most, 2 * len(plan))
    return pl.pallas_call(
        functools.partial(reduce_kernel, plans, shards, len(grads)),
        out_shape=outs,
        in_specs=[pl.BlockSpec(memory_space=pltpu.VMEM)] * len(grads),
        out_specs=[pl.BlockSpec(memory_space=pltpu.VMEM)] * len(grads),
        scratch_shapes=lands
        + [
            pltpu.SemaphoreType.DMA((len(grads), most)),
            pltpu.SemaphoreType.DMA((len(grads), most)),
        ],
        compiler_params=pltpu.CompilerParams(
            collective_id=1, has_side_effects=True, vmem_limit_bytes=VMEM_LIMIT
        ),
    )(*grads)


def body(
    shards,
    reps,
    inputs,
    segments,
    cotangent,
    norm1_gain,
    w_query,
    w_key,
    w_value,
    w_out,
    norm2_gain,
    w_gate,
    w_up,
    w_down,
):
    share = 4 if reps % 4 == 0 else 1
    w_attn = jnp.concatenate([w_query, w_key, w_value, w_out], axis=1)
    w_gain = jnp.zeros((16, norm1_gain.shape[0]), norm1_gain.dtype)
    w_gain = w_gain.at[0].set(norm1_gain).at[1].set(norm2_gain)
    nq, nk = w_query.shape[1], w_key.shape[1]
    w_all = gather_weights(
        [w_attn, w_gate, w_up, w_down, w_gain], [2, 2, 2, 1, None], shards, share
    )
    wa, wg, wu, wd = [w.reshape(-1, w.shape[2]) for w in w_all[:4]]
    gain_one, gain_two = w_all[4][:, 0].reshape(-1), w_all[4][:, 1].reshape(-1)
    wq, wk, wv = wa[:, :nq], wa[:, nq : nq + nk], wa[:, nq + nk : nq + 2 * nk]
    wo = wa[:, nq + 2 * nk :]
    x = inputs[0].astype(jnp.float32)
    seg_row = segments[0]
    count = x.shape[0]
    width = x.shape[1]
    kv_heads = wk.shape[1] // HEAD_DIM
    heads = wq.shape[1] // HEAD_DIM
    group = heads // kv_heads
    scale = HEAD_DIM ** (-0.5)
    cosine, sine = rope_tables(seg_row, HEAD_DIM)
    index = jnp.arange(count)
    allowed = (seg_row[:, None] == seg_row[None, :]) & (index[:, None] >= index[None, :])
    g_one = gain_one.astype(jnp.float32)
    r_one = lax.rsqrt(jnp.mean(x * x, axis=1, keepdims=True) + eps)
    h_one = (x * r_one * g_one).astype(jnp.bfloat16)
    q_lin = jnp.dot(h_one, wq, preferred_element_type=jnp.float32)
    k_lin = jnp.dot(h_one, wk, preferred_element_type=jnp.float32)
    values = (
        jnp.dot(h_one, wv, preferred_element_type=jnp.float32)
        .astype(jnp.bfloat16)
        .reshape(count, kv_heads, HEAD_DIM)
    )
    queries = (
        rotate(q_lin.reshape(count, heads, HEAD_DIM), cosine, sine, 1.0)
        .astype(jnp.bfloat16)
        .reshape(count, kv_heads, group, HEAD_DIM)
    )
    keys = rotate(k_lin.reshape(count, kv_heads, HEAD_DIM), cosine, sine, 1.0).astype(jnp.bfloat16)
    scores = attention_scores(queries, keys, allowed, scale)
    top = jnp.max(scores, axis=3, keepdims=True)
    expo = jnp.exp(scores - top)
    total = jnp.sum(expo, axis=3, keepdims=True)
    lse = top + jnp.log(total)
    probs = (expo / total).astype(jnp.bfloat16)
    mixed = jnp.einsum("kgts,skd->tkgd", probs, values, preferred_element_type=jnp.float32)
    mixed_b = mixed.reshape(count, width).astype(jnp.bfloat16)
    y_one = x + jnp.dot(mixed_b, wo, preferred_element_type=jnp.float32)
    g_two = gain_two.astype(jnp.float32)
    r_two = lax.rsqrt(jnp.mean(y_one * y_one, axis=1, keepdims=True) + eps)
    h_two = (y_one * r_two * g_two).astype(jnp.bfloat16)
    gate = jnp.dot(h_two, wg, preferred_element_type=jnp.float32)
    up_val = jnp.dot(h_two, wu, preferred_element_type=jnp.float32)
    sigm = jax.nn.sigmoid(gate)
    hidden = (gate * sigm * up_val).astype(jnp.bfloat16)
    output = y_one + jnp.dot(hidden, wd, preferred_element_type=jnp.float32)
    bq, bk, bv, bo, bg, bu, bd = wq, wk, wv, wo, wg, wu, wd
    d_out = cotangent[0].astype(jnp.float32)
    d_out_b = d_out.astype(jnp.bfloat16)
    grad_down = jnp.einsum("tf,td->fd", hidden, d_out_b, preferred_element_type=jnp.float32)
    d_hidden = jnp.einsum("td,fd->tf", d_out_b, bd, preferred_element_type=jnp.float32)
    d_up = (d_hidden * gate * sigm).astype(jnp.bfloat16)
    d_gate = (d_hidden * up_val * sigm * (1.0 + gate * (1.0 - sigm))).astype(jnp.bfloat16)
    grad_gate = jnp.einsum("td,tf->df", h_two, d_gate, preferred_element_type=jnp.float32)
    grad_up = jnp.einsum("td,tf->df", h_two, d_up, preferred_element_type=jnp.float32)
    d_h_two = jnp.einsum("tf,df->td", d_gate, bg, preferred_element_type=jnp.float32) + jnp.einsum(
        "tf,df->td", d_up, bu, preferred_element_type=jnp.float32
    )
    grad_gain_two = jnp.sum(d_h_two * y_one * r_two, axis=0)
    u_two = d_h_two * g_two
    d_y_one = (
        d_out + r_two * u_two - y_one * r_two**3 * jnp.mean(u_two * y_one, axis=1, keepdims=True)
    )
    d_attn = d_y_one.astype(jnp.bfloat16)
    grad_wo = jnp.einsum("td,te->de", mixed_b, d_attn, preferred_element_type=jnp.float32)
    d_mixed = (
        jnp.einsum("te,de->td", d_attn, bo, preferred_element_type=jnp.float32)
        .astype(jnp.bfloat16)
        .reshape(count, kv_heads, group, HEAD_DIM)
    )
    probs_f = jnp.exp(attention_scores(queries, keys, allowed, scale) - lse)
    probs_b = probs_f.astype(jnp.bfloat16)
    d_probs = jnp.einsum("tkgd,skd->kgts", d_mixed, values, preferred_element_type=jnp.float32)
    delta = jnp.sum(d_probs * probs_f, axis=3, keepdims=True)
    d_scores = (probs_f * (d_probs - delta)).astype(jnp.bfloat16)
    d_queries = (
        jnp.einsum("kgts,skd->tkgd", d_scores, keys, preferred_element_type=jnp.float32) * scale
    )
    d_keys = (
        jnp.einsum("kgts,tkgd->skd", d_scores, queries, preferred_element_type=jnp.float32) * scale
    )
    d_values = jnp.einsum("kgts,tkgd->skd", probs_b, d_mixed, preferred_element_type=jnp.float32)
    dq_b = (
        rotate(d_queries.reshape(count, heads, HEAD_DIM), cosine, sine, -1.0)
        .reshape(count, width)
        .astype(jnp.bfloat16)
    )
    dk_b = (
        rotate(d_keys, cosine, sine, -1.0).reshape(count, kv_heads * HEAD_DIM).astype(jnp.bfloat16)
    )
    dv_b = d_values.reshape(count, kv_heads * HEAD_DIM).astype(jnp.bfloat16)
    grad_wq = jnp.einsum("td,te->de", h_one, dq_b, preferred_element_type=jnp.float32)
    grad_wk = jnp.einsum("td,te->de", h_one, dk_b, preferred_element_type=jnp.float32)
    grad_wv = jnp.einsum("td,te->de", h_one, dv_b, preferred_element_type=jnp.float32)
    d_h_one = jnp.einsum("te,de->td", dq_b, bq, preferred_element_type=jnp.float32)
    d_h_one = d_h_one + jnp.einsum("te,de->td", dk_b, bk, preferred_element_type=jnp.float32)
    d_h_one = d_h_one + jnp.einsum("te,de->td", dv_b, bv, preferred_element_type=jnp.float32)
    grad_gain_one = jnp.sum(d_h_one * x * r_one, axis=0)
    u_one = d_h_one * g_one
    d_x = d_y_one + r_one * u_one - x * r_one**3 * jnp.mean(u_one * x, axis=1, keepdims=True)
    low = jnp.bfloat16
    g_attn = jnp.concatenate([grad_wq, grad_wk, grad_wv, grad_wo], axis=1)
    g_gains = jnp.zeros((1, 8, width), jnp.float32)
    g_gains = g_gains.at[0, 0].set(grad_gain_one).at[0, 1].set(grad_gain_two)
    parts = [
        g.astype(low).reshape(shards, -1, g.shape[1])
        for g in (grad_down, grad_gate, grad_up, g_attn)
    ]
    sums = reduce_grads(parts + [g_gains], [True] * 4 + [False], shards, reps)
    t_down, t_gate, t_up, t_attn = [t[0].astype(jnp.float32) for t in sums[:4]]
    g_gains = sums[4][0, :2]
    own = width // shards
    g_gains = lax.dynamic_slice_in_dim(g_gains, lax.axis_index("shard") * own, own, 1)
    return (
        output.astype(low)[None],
        d_x.astype(low)[None],
        g_gains[0],
        t_attn[:, :nq],
        t_attn[:, nq : nq + nk],
        t_attn[:, nq + nk : nq + 2 * nk],
        t_attn[:, nq + 2 * nk :],
        g_gains[1],
        t_gate,
        t_up,
        t_down,
    )


def solution(mesh):
    return jax.shard_map(
        functools.partial(body, mesh.shape["shard"], mesh.shape["rep"]),
        mesh=mesh,
        in_specs=(
            P(("rep", "shard"), None, None),
            P(("rep", "shard"), None),
            P(("rep", "shard"), None, None),
            P("shard"),
            P("shard", None),
            P("shard", None),
            P("shard", None),
            P("shard", None),
            P("shard"),
            P("shard", None),
            P("shard", None),
            P("shard", None),
        ),
        out_specs=(
            P(("rep", "shard"), None, None),
            P(("rep", "shard"), None, None),
            P("shard"),
            P("shard", None),
            P("shard", None),
            P("shard", None),
            P("shard", None),
            P("shard"),
            P("shard", None),
            P("shard", None),
            P("shard", None),
        ),
        check_vma=False,
    )
```

```python
import functools
import math

import jax
import jax.numpy as jnp
from jax import lax
from jax.experimental import pallas as pl
from jax.experimental.pallas import tpu as pltpu
from jax.sharding import PartitionSpec as P

HEAD_DIM = 64
MESH = pl.DeviceIdType.MESH
VMEM_LIMIT = 48 * 1024 * 1024


eps = 1e-05
rope_base = 100000.0


def rope_tables(seg_row, head_dim):
    count = seg_row.shape[0]
    index = jnp.arange(count, dtype=jnp.int32)
    before = jnp.concatenate([jnp.full((1,), -1, jnp.int32), seg_row[:-1]])
    starts = jnp.where(seg_row != before, index, jnp.zeros_like(index))
    place = (index - lax.cummax(starts, axis=0)).astype(jnp.float32)
    half = head_dim // 2
    freqs = jnp.exp(jnp.arange(half, dtype=jnp.float32) * (-2.0 * math.log(rope_base) / head_dim))
    angle = place[:, None] * freqs[None, :]
    return (jnp.cos(angle), jnp.sin(angle))


def rotate(values, cosine, sine, sign):
    half = values.shape[-1] // 2
    first = values[..., :half]
    second = values[..., half:]
    cos_b = cosine[:, None, :]
    sin_b = sine[:, None, :] * sign
    return jnp.concatenate(
        [first * cos_b - second * sin_b, second * cos_b + first * sin_b], axis=-1
    )


def attention_scores(queries, keys, allowed, scale):
    dots = jnp.einsum("tkgd,skd->kgts", queries, keys, preferred_element_type=jnp.float32) * scale
    return jnp.where(allowed[None, None], dots, -1e30)


def bits_of(size):
    return [1 << b for b in range(size.bit_length() - 1)]


def flipped(index, bit):
    return index + bit - 2 * bit * ((index // bit) % 2)


def greet(partners):
    barrier = pltpu.get_barrier_semaphore()
    for partner in partners:
        pl.semaphore_signal(barrier, inc=1, device_id=partner, device_id_type=MESH)
    pl.semaphore_wait(barrier, len(partners))


def gather_kernel(shards, share, dims, *refs):
    count = len(dims)
    blocks, outs = refs[:count], refs[count : 2 * count]
    send, recv, local = refs[2 * count :]
    r, s = lax.axis_index("rep"), lax.axis_index("shard")
    bits = list(reversed(bits_of(share)))
    others = [lax.rem(s + t, shards) for t in range(1, shards)]
    back = [lax.rem(s + shards - t, shards) for t in range(1, shards)]
    greet([(r, o) for o in others] + [(flipped(r, bit), s) for bit in bits])

    def part(ref, dim, owner):
        if dim is None:
            return (slice(None), slice(None))
        size = ref.shape[dim - (3 - len(ref.shape))] // share
        cut = pl.ds(pl.multiple_of(owner * size, size), size)
        return (cut, slice(None)) if dim == 1 else (slice(None), cut)

    held = {}
    copies, stays = [], []
    for a in range(count):
        own = pltpu.make_async_copy(blocks[a], outs[a].at[s], local.at[a])
        own.start()
        stays.append(own)
        held[a] = [lax.rem(r, share)]
        for t in range(1, shards):
            cut = part(blocks[a], dims[a], held[a][0])
            go = pltpu.make_async_remote_copy(
                src_ref=blocks[a].at[cut],
                dst_ref=outs[a].at[(s,) + cut],
                send_sem=send.at[a, t - 1, 0],
                recv_sem=recv.at[a, t - 1, 0],
                device_id=(r, others[t - 1]),
                device_id_type=MESH,
            )
            go.start()
            held[a, t] = [go]
    pending = {}
    for tick in range(count + len(bits)):
        for a in range(count):
            level = tick - a
            if dims[a] is None or not 0 <= level < len(bits):
                continue
            bit = bits[level]
            fresh = []
            for t in range(1, shards):
                arrived = held[a, t] if level == 0 else pending[a, t]
                for go in arrived:
                    go.wait_recv()
                now = []
                for j in range(1 << level):
                    owner = held[a][j]
                    cut = part(blocks[a], dims[a], owner)
                    where = outs[a].at[(back[t - 1],) + cut]
                    go = pltpu.make_async_remote_copy(
                        src_ref=where,
                        dst_ref=where,
                        send_sem=send.at[a, t - 1, (1 << level) + j],
                        recv_sem=recv.at[a, t - 1, (1 << level) + j],
                        device_id=(flipped(r, bit), s),
                        device_id_type=MESH,
                    )
                    go.start()
                    now.append(go)
                pending[a, t] = now
                copies.extend(arrived)
            held[a] = held[a] + [flipped(o, bit) for o in held[a]]
    for a in range(count):
        for t in range(1, shards):
            last = pending.get((a, t), held[a, t])
            for go in last:
                go.wait_recv()
            copies.extend(last)
    for go in copies:
        go.wait_send()
    for own in stays:
        own.wait()


def gather_weights(blocks, dims, shards, share):
    return pl.pallas_call(
        functools.partial(gather_kernel, shards, share, dims),
        out_shape=[jax.ShapeDtypeStruct((shards,) + b.shape, b.dtype) for b in blocks],
        in_specs=[pl.BlockSpec(memory_space=pltpu.VMEM)] * len(blocks),
        out_specs=[pl.BlockSpec(memory_space=pltpu.VMEM)] * len(blocks),
        scratch_shapes=[
            pltpu.SemaphoreType.DMA((len(blocks), max(1, shards - 1), share)),
            pltpu.SemaphoreType.DMA((len(blocks), max(1, shards - 1), share)),
            pltpu.SemaphoreType.DMA((len(blocks),)),
        ],
        compiler_params=pltpu.CompilerParams(
            collective_id=0, has_side_effects=True, vmem_limit_bytes=VMEM_LIMIT
        ),
    )(*blocks)


def plan_of(shape, shards, reps, splits, turn):
    rep_bits, shard_bits = bits_of(reps), list(reversed(bits_of(shards)))
    size = list(shape)
    order = [("rep", b) for b in rep_bits]
    if turn in "ZWU" and len(order) > 3:
        order[1], order[2] = order[2], order[1]
    first = {"Y": 1, "W": 1, "X": 2, "Z": 2, "V": 3, "U": 3}[turn]
    order[first:first] = [("shard", b) for b in shard_bits]
    steps = []
    for n, (axis, bit) in enumerate(order):
        dim = None
        if splits and axis == "shard":
            dim = 0
        elif splits and n < len(order) - 1:
            if size[1] % 32 == 0 and (size[2] % 256 != 0 or n == 0):
                dim = 1
            elif size[2] % 256 == 0:
                dim = 2
        if dim is not None:
            size[dim] //= 2
        steps.append((axis, bit, dim, tuple(size)))
    return steps


def piece_of(ref, dim, base, size):
    if dim is None:
        return ref
    cut = [slice(None)] * 3
    cut[dim] = pl.ds(base, size)
    return ref.at[tuple(cut)]


def reduce_kernel(plans, pieces, arrays, *refs):
    count = len(pieces)
    grads = [piece_of(refs[a], *cut) for a, *cut in pieces]
    outs = [piece_of(refs[arrays + a], *cut) for a, *cut in pieces]
    refs = refs[2 * arrays :]
    send, recv = refs[-2:]
    lands, at = [], 0
    for plan in plans:
        lands.append(refs[at : at + len(plan)])
        at += len(plan)
    r, s = lax.axis_index("rep"), lax.axis_index("shard")
    index = {"rep": r, "shard": s}

    def partner(axis, bit):
        return (flipped(r, bit), s) if axis == "rep" else (r, flipped(s, bit))

    greet([partner(axis, bit) for axis, bit, _, _ in plans[0]])

    def half(shape, dim, which):
        cut = [slice(None)] * 3
        size = shape[dim] // 2
        start = which * size
        cut[dim] = pl.ds(start if dim == 0 else pl.multiple_of(start, size), size)
        return tuple(cut)

    waits, free, clock = [], {}, [0.0]

    def start(c, n, src, dst, axis, bit):
        go = pltpu.make_async_remote_copy(
            src_ref=src,
            dst_ref=dst,
            send_sem=send.at[c, n],
            recv_sem=recv.at[c, n],
            device_id=partner(axis, bit),
            device_id_type=MESH,
        )
        go.start()
        waits.append(go)
        link = (axis, bit)
        rate = 300e3 if link == ("rep", 1) else 50e3
        begin = max(clock[0], free.get(link, 0.0))
        free[link] = begin + math.prod(dst.shape) * 2 / rate
        return go, free[link] + 1.5

    def stream(c):
        plan, cur = plans[c], grads[c]
        offset = [0, 0, 0]
        shape = cur.shape
        n = 0
        for step, (axis, bit, dim, after) in enumerate(plan):
            land = lands[c][step]
            on = (index[axis] // bit) % 2
            if dim is None:
                go, due = start(c, n, cur, land, axis, bit)
                yield due
                go.wait_recv()
                land[...] = cur[...] + land[...]
            else:
                theirs = half(shape, dim, 1 - on)
                mine = half(shape, dim, on)
                go, due = start(c, n, cur.at[theirs], land, axis, bit)
                yield due
                go.wait_recv()
                land[...] = cur[mine] + land[...]
                if axis == "rep":
                    offset[dim] = offset[dim] + on * after[dim]
            cur, shape = land, after
            n += 1
        out = outs[c]

        def place(offset, size):
            cut = []
            for d in (1, 2):
                if size[d] == out.shape[d]:
                    cut.append(slice(None))
                else:
                    unit = 16 if d == 1 else 128
                    cut.append(pl.ds(pl.multiple_of(offset[d], unit), size[d]))
            return (slice(None),) + tuple(cut)

        size = list(shape)
        out[place(offset, size)] = cur[...]
        for axis, bit, dim, after in reversed(plan):
            if axis == "shard" or dim is None:
                continue
            block = out.at[place(offset, size)]
            go, due = start(c, n, block, block, axis, bit)
            yield due
            go.wait_recv()
            on = (index[axis] // bit) % 2
            offset[dim] = offset[dim] - on * after[dim]
            size[dim] *= 2
            n += 1

    streams = [stream(c) for c in range(count)]
    due = [(next(one), c) for c, one in enumerate(streams)]
    while due:
        due.sort()
        clock[0], c = due.pop(0)
        then = next(streams[c], None)
        if then is not None:
            due.append((then, c))
    for go in waits:
        go.wait_send()


TURNS = "WUUYYYYYVZZY"


def reduce_grads(grads, cuts, shards, reps):
    plans, pieces, lands, outs = [], [], [], []
    for a, (g, dim) in enumerate(zip(grads, cuts)):
        outs.append(jax.ShapeDtypeStruct((1 if dim else g.shape[0],) + g.shape[1:], g.dtype))
        number = 3 if dim else 1
        for n in range(number):
            shape = list(g.shape)
            if dim:
                shape[dim] //= number
            turn = TURNS[len(pieces) % len(TURNS)]
            plan = plan_of(tuple(shape), shards, reps, dim is not None, turn)
            size = shape[dim] if dim else 0
            pieces.append((a, dim, n * size, size))
            plans.append(plan)
            lands += [pltpu.VMEM(after, g.dtype) for _, _, _, after in plan]
    most = max(2 * len(plan) for plan in plans)
    return pl.pallas_call(
        functools.partial(reduce_kernel, plans, pieces, len(grads)),
        out_shape=outs,
        in_specs=[pl.BlockSpec(memory_space=pltpu.VMEM)] * len(grads),
        out_specs=[pl.BlockSpec(memory_space=pltpu.VMEM)] * len(grads),
        scratch_shapes=lands
        + [
            pltpu.SemaphoreType.DMA((len(pieces), most)),
            pltpu.SemaphoreType.DMA((len(pieces), most)),
        ],
        compiler_params=pltpu.CompilerParams(
            collective_id=1, has_side_effects=True, vmem_limit_bytes=VMEM_LIMIT
        ),
    )(*grads)


def body(
    shards,
    reps,
    inputs,
    segments,
    cotangent,
    norm1_gain,
    w_query,
    w_key,
    w_value,
    w_out,
    norm2_gain,
    w_gate,
    w_up,
    w_down,
):
    share = 4 if reps % 4 == 0 else 1
    w_attn = jnp.concatenate([w_query, w_key, w_value, w_out], axis=1)
    w_gain = jnp.zeros((16, norm1_gain.shape[0]), norm1_gain.dtype)
    w_gain = w_gain.at[0].set(norm1_gain).at[1].set(norm2_gain)
    nq, nk = w_query.shape[1], w_key.shape[1]
    w_all = gather_weights(
        [w_attn, w_gate, w_up, w_down, w_gain], [2, 2, 2, 1, None], shards, share
    )
    wa, wg, wu, wd = [w.reshape(-1, w.shape[2]) for w in w_all[:4]]
    gain_one, gain_two = w_all[4][:, 0].reshape(-1), w_all[4][:, 1].reshape(-1)
    wq, wk, wv = wa[:, :nq], wa[:, nq : nq + nk], wa[:, nq + nk : nq + 2 * nk]
    wo = wa[:, nq + 2 * nk :]
    x = inputs[0].astype(jnp.float32)
    seg_row = segments[0]
    count = x.shape[0]
    width = x.shape[1]
    kv_heads = wk.shape[1] // HEAD_DIM
    heads = wq.shape[1] // HEAD_DIM
    group = heads // kv_heads
    scale = HEAD_DIM ** (-0.5)
    cosine, sine = rope_tables(seg_row, HEAD_DIM)
    index = jnp.arange(count)
    allowed = (seg_row[:, None] == seg_row[None, :]) & (index[:, None] >= index[None, :])
    g_one = gain_one.astype(jnp.float32)
    r_one = lax.rsqrt(jnp.mean(x * x, axis=1, keepdims=True) + eps)
    h_one = (x * r_one * g_one).astype(jnp.bfloat16)
    q_lin = jnp.dot(h_one, wq, preferred_element_type=jnp.float32)
    k_lin = jnp.dot(h_one, wk, preferred_element_type=jnp.float32)
    values = (
        jnp.dot(h_one, wv, preferred_element_type=jnp.float32)
        .astype(jnp.bfloat16)
        .reshape(count, kv_heads, HEAD_DIM)
    )
    queries = (
        rotate(q_lin.reshape(count, heads, HEAD_DIM), cosine, sine, 1.0)
        .astype(jnp.bfloat16)
        .reshape(count, kv_heads, group, HEAD_DIM)
    )
    keys = rotate(k_lin.reshape(count, kv_heads, HEAD_DIM), cosine, sine, 1.0).astype(jnp.bfloat16)
    scores = attention_scores(queries, keys, allowed, scale)
    top = jnp.max(scores, axis=3, keepdims=True)
    expo = jnp.exp(scores - top)
    total = jnp.sum(expo, axis=3, keepdims=True)
    lse = top + jnp.log(total)
    probs = (expo / total).astype(jnp.bfloat16)
    mixed = jnp.einsum("kgts,skd->tkgd", probs, values, preferred_element_type=jnp.float32)
    mixed_b = mixed.reshape(count, width).astype(jnp.bfloat16)
    y_one = x + jnp.dot(mixed_b, wo, preferred_element_type=jnp.float32)
    g_two = gain_two.astype(jnp.float32)
    r_two = lax.rsqrt(jnp.mean(y_one * y_one, axis=1, keepdims=True) + eps)
    h_two = (y_one * r_two * g_two).astype(jnp.bfloat16)
    gate = jnp.dot(h_two, wg, preferred_element_type=jnp.float32)
    up_val = jnp.dot(h_two, wu, preferred_element_type=jnp.float32)
    sigm = jax.nn.sigmoid(gate)
    hidden = (gate * sigm * up_val).astype(jnp.bfloat16)
    output = y_one + jnp.dot(hidden, wd, preferred_element_type=jnp.float32)
    bq, bk, bv, bo, bg, bu, bd = wq, wk, wv, wo, wg, wu, wd
    d_out = cotangent[0].astype(jnp.float32)
    d_out_b = d_out.astype(jnp.bfloat16)
    grad_down = jnp.einsum("tf,td->fd", hidden, d_out_b, preferred_element_type=jnp.float32)
    d_hidden = jnp.einsum("td,fd->tf", d_out_b, bd, preferred_element_type=jnp.float32)
    d_up = (d_hidden * gate * sigm).astype(jnp.bfloat16)
    d_gate = (d_hidden * up_val * sigm * (1.0 + gate * (1.0 - sigm))).astype(jnp.bfloat16)
    grad_gate = jnp.einsum("td,tf->df", h_two, d_gate, preferred_element_type=jnp.float32)
    grad_up = jnp.einsum("td,tf->df", h_two, d_up, preferred_element_type=jnp.float32)
    d_h_two = jnp.einsum("tf,df->td", d_gate, bg, preferred_element_type=jnp.float32) + jnp.einsum(
        "tf,df->td", d_up, bu, preferred_element_type=jnp.float32
    )
    grad_gain_two = jnp.sum(d_h_two * y_one * r_two, axis=0)
    u_two = d_h_two * g_two
    d_y_one = (
        d_out + r_two * u_two - y_one * r_two**3 * jnp.mean(u_two * y_one, axis=1, keepdims=True)
    )
    d_attn = d_y_one.astype(jnp.bfloat16)
    grad_wo = jnp.einsum("td,te->de", mixed_b, d_attn, preferred_element_type=jnp.float32)
    d_mixed = (
        jnp.einsum("te,de->td", d_attn, bo, preferred_element_type=jnp.float32)
        .astype(jnp.bfloat16)
        .reshape(count, kv_heads, group, HEAD_DIM)
    )
    probs_f = jnp.exp(attention_scores(queries, keys, allowed, scale) - lse)
    probs_b = probs_f.astype(jnp.bfloat16)
    d_probs = jnp.einsum("tkgd,skd->kgts", d_mixed, values, preferred_element_type=jnp.float32)
    delta = jnp.sum(d_probs * probs_f, axis=3, keepdims=True)
    d_scores = (probs_f * (d_probs - delta)).astype(jnp.bfloat16)
    d_queries = (
        jnp.einsum("kgts,skd->tkgd", d_scores, keys, preferred_element_type=jnp.float32) * scale
    )
    d_keys = (
        jnp.einsum("kgts,tkgd->skd", d_scores, queries, preferred_element_type=jnp.float32) * scale
    )
    d_values = jnp.einsum("kgts,tkgd->skd", probs_b, d_mixed, preferred_element_type=jnp.float32)
    dq_b = (
        rotate(d_queries.reshape(count, heads, HEAD_DIM), cosine, sine, -1.0)
        .reshape(count, width)
        .astype(jnp.bfloat16)
    )
    dk_b = (
        rotate(d_keys, cosine, sine, -1.0).reshape(count, kv_heads * HEAD_DIM).astype(jnp.bfloat16)
    )
    dv_b = d_values.reshape(count, kv_heads * HEAD_DIM).astype(jnp.bfloat16)
    grad_wq = jnp.einsum("td,te->de", h_one, dq_b, preferred_element_type=jnp.float32)
    grad_wk = jnp.einsum("td,te->de", h_one, dk_b, preferred_element_type=jnp.float32)
    grad_wv = jnp.einsum("td,te->de", h_one, dv_b, preferred_element_type=jnp.float32)
    d_h_one = jnp.einsum("te,de->td", dq_b, bq, preferred_element_type=jnp.float32)
    d_h_one = d_h_one + jnp.einsum("te,de->td", dk_b, bk, preferred_element_type=jnp.float32)
    d_h_one = d_h_one + jnp.einsum("te,de->td", dv_b, bv, preferred_element_type=jnp.float32)
    grad_gain_one = jnp.sum(d_h_one * x * r_one, axis=0)
    u_one = d_h_one * g_one
    d_x = d_y_one + r_one * u_one - x * r_one**3 * jnp.mean(u_one * x, axis=1, keepdims=True)
    low = jnp.bfloat16
    g_attn = jnp.concatenate([grad_wq, grad_wk, grad_wv, grad_wo], axis=1)
    g_gains = jnp.zeros((1, 8, width), jnp.float32)
    g_gains = g_gains.at[0, 0].set(grad_gain_one).at[0, 1].set(grad_gain_two)
    parts = [
        g.astype(low).reshape(shards, -1, g.shape[1])
        for g in (grad_down, grad_gate, grad_up, g_attn)
    ]
    sums = reduce_grads(parts + [g_gains], [1, 2, 2, 2, None], shards, reps)
    t_down, t_gate, t_up, t_attn = [t[0].astype(jnp.float32) for t in sums[:4]]
    g_gains = sums[4][0, :2]
    own = width // shards
    g_gains = lax.dynamic_slice_in_dim(g_gains, lax.axis_index("shard") * own, own, 1)
    return (
        output.astype(low)[None],
        d_x.astype(low)[None],
        g_gains[0],
        t_attn[:, :nq],
        t_attn[:, nq : nq + nk],
        t_attn[:, nq + nk : nq + 2 * nk],
        t_attn[:, nq + 2 * nk :],
        g_gains[1],
        t_gate,
        t_up,
        t_down,
    )


def solution(mesh):
    return jax.shard_map(
        functools.partial(body, mesh.shape["shard"], mesh.shape["rep"]),
        mesh=mesh,
        in_specs=(
            P(("rep", "shard"), None, None),
            P(("rep", "shard"), None),
            P(("rep", "shard"), None, None),
            P("shard"),
            P("shard", None),
            P("shard", None),
            P("shard", None),
            P("shard", None),
            P("shard"),
            P("shard", None),
            P("shard", None),
            P("shard", None),
        ),
        out_specs=(
            P(("rep", "shard"), None, None),
            P(("rep", "shard"), None, None),
            P("shard"),
            P("shard", None),
            P("shard", None),
            P("shard", None),
            P("shard", None),
            P("shard"),
            P("shard", None),
            P("shard", None),
            P("shard", None),
        ),
        check_vma=False,
    )
```
